256 devices in a mesh: cp: 32 (over x_hi, z, core), tp: 4 (over y), dp: 2 (over x_lo).
Axes of the slice: x: 4 (x_hi: 2, x_lo: 2; x = x_hi * 2 + x_lo), y: 4, z: 8, core: 2. Of those that a mesh axis runs over, the one named last changes fastest.
Arguments:
- query_rows: bfloat16 [2, 4096, 6144], P('dp', 'cp', 'tp'), may hold values from -8 to 8
- key_rows: bfloat16 [2, 4096, 1024], P('dp', 'cp', 'tp'), may hold values from -8 to 8
- value_rows: bfloat16 [2, 4096, 1024], P('dp', 'cp', 'tp'), may hold values from -6 to 6
- attention_out: bfloat16 [2, 4096, 6144], P('dp', 'cp', 'tp'), may hold values from -6 to 6
- output_grad: bfloat16 [2, 4096, 6144], P('dp', 'cp', 'tp'), may hold values from -24 to 24
- log_norms: float32 [2, 4096, 48], P('dp', 'cp', 'tp')
- moe_grad: bfloat16 [2, 4096, 6144], P('dp', 'cp', 'tp'), may hold values from -6 to 6
- expert_ids: int32 [2, 4096, 2], P('dp', 'cp'), may hold values from 0 to 7, all different within a row; in each aligned block of 128 rows (0 to 127, 128 to 255, ..., all dimensions but the last counted through in order) at most 48 rows name the same one
- route_weight: int32 [2, 4096, 2], P('dp', 'cp'), may hold values from 1 to 32767
- hidden_act: bfloat16 [2, 1536, 65536], P('dp', 'tp', 'cp'), may hold values from -0.1875 to 0.1875
Outputs:
- query_grad: bfloat16 [2, 4096, 6144], P('dp', 'cp', 'tp')
- key_grad: bfloat16 [2, 4096, 1024], P('dp', 'cp', 'tp')
- value_grad: bfloat16 [2, 4096, 1024], P('dp', 'cp', 'tp')
- down_grad: bfloat16 [65536, 6144], P(('cp', 'dp'), 'tp')
The draws below stay inside these ranges and needn't reach their ends.
Inputs may be any that keep to these rules, and one draw needn't show every extreme that they name: `expert_ids`: in each aligned block of 128 tokens of a sequence no expert is named by more than 48 tokens, a bound that some block reaches; a token names 2 different experts.
All inputs are finite; a program needn't handle non-finite values.
Results may differ from the reference program's by a relative error of at most 0.0052.
Values may be sent and summed in bfloat16 or wider, within the bound.
No kernel may reach another device: no remote copies, remote signals or barrier semaphores. Data moves between devices by JAX's collectives and lax.ppermute only.
A program may use at most 128 MiB of HBM per device.

```python
import math
import jax
import jax.numpy as jnp
import numpy as np
from jax import lax

D = 6144
HEADS = 48
KV_HEADS = 8
HEAD_DIM = 128
F = 8192
TOP = 2
TOK_DEV = 128
EXPERTS = 8
CAP = 48
SLOTS = 1536
F_ALL = 65536
SEQS = 2
LENGTH = 4096
N_CP = 32


def draw_log_norms(key, part):
    key = jax.random.fold_in(key, 7)
    jitter = jax.random.uniform(key, (SEQS, LENGTH, HEADS), jnp.float32, -0.3, 0.3)
    position = jnp.arange(LENGTH, dtype=jnp.float32)
    return jnp.log(position + 1.0)[None, :, None] + 2.5 + jitter


def plant(values, key, low, largest):
    longest = values.shape.index(max(values.shape))
    spots = []
    for shift in (0, 1):
        where = [jax.random.randint(jax.random.fold_in(key, axis), (), 0, length) for axis, length in enumerate(values.shape)]
        where[longest] = (where[longest] + shift) % values.shape[longest]
        spots.append(tuple(where))
    return values.at[spots[0]].set(low).at[spots[1]].set(largest)


def shard_levels(rng, shape, shards, smallest, top_value):
    gain = 1.0
    for dim, blocks in shards:
        steps = jax.random.uniform(jax.random.fold_in(jax.random.fold_in(rng, 6), dim), (blocks,), jnp.float32, smallest / len(shards), top_value / len(shards))
        gain = gain * jnp.repeat(jnp.exp(steps), shape[dim] // blocks).reshape((-1,) + (1,) * (len(shape) - 1 - dim))
    return gain


def deal_out(rng, own, number, rows, count, top, bound, skew):
    ranking = jax.random.permutation(rng, count)
    crowded, common = portions_of(count, rows * top, bound, skew, True), portions_of(count, rows * top, bound, skew, False)
    places = jnp.arange(count)

    def named(sizes, turn):
        used = int((sizes > 0).sum())
        fixed = max(1, used // 4)
        shifted = fixed + (places - fixed + turn * (used - fixed)) % max(1, count - fixed)
        return jnp.zeros((count,), jnp.int32).at[ranking[jnp.where(places < fixed, places, shifted)]].set(jnp.asarray(sizes, jnp.int32))

    sizes = jnp.where(number % 4 == 0, named(crowded, number // 4), named(common, number - number // 4 - 1))
    mixed = jax.random.permutation(jax.random.fold_in(own, 3), count)
    donor, sink = mixed[0:count // 2 * 2:2], mixed[1:count // 2 * 2:2]
    room = jnp.minimum(sizes[donor] - 1, bound - sizes[sink]) // 2
    room = jnp.where((donor == ranking[0]) | (sink == ranking[0]) | (sizes[sink] == 0), 0, jnp.maximum(room, 0))
    shifted = jax.random.randint(jax.random.fold_in(own, 4), (count // 2,), 0, 1 << 20) % (room + 1)
    sizes = sizes.at[donor].add(-shifted).at[sink].add(shifted)
    labels = jnp.searchsorted(jnp.cumsum(sizes), jnp.arange(rows * top), side="right").astype(jnp.int32)
    table = labels.reshape(top, rows).T
    table = table[jax.random.permutation(jax.random.fold_in(own, 1), rows)]
    turn = jax.random.randint(jax.random.fold_in(own, 2), (rows, 1), 0, top)
    return jnp.take_along_axis(table, (jnp.arange(top)[None, :] + turn) % top, axis=1)


def portions_of(count, total, most, lean, full):
    portions = [(1 << 20) // math.isqrt(grade ** lean) + 1 for grade in range(1, count + 1)]
    largest = most if full else min(most, max(-(-total // count), total * portions[0] // sum(portions)))
    least = 1 if total - largest >= count - 1 else 0
    given, surplus = [largest] + [least] * (count - 1), total - largest - least * (count - 1)
    while surplus > 0:
        movable = [i for i in range(1, count) if given[i] < largest] or [i for i in range(1, count) if given[i] < most]
        pool, remaining = sum([portions[i] for i in movable]), surplus
        for i in movable:
            more = min(most - given[i], max(1, remaining * portions[i] // pool), surplus)
            given[i] = given[i] + more
            surplus = surplus - more
    return np.array(given)


def gaussian(rng, dims, spread, limit, pieces=(), kind=jnp.bfloat16):
    values = jax.random.normal(rng, dims, jnp.float32) * spread
    if len(pieces) > 0:
        values = shard_levels(rng, dims, pieces, -0.22, 0.18) * values
    return jnp.clip(values, min=-limit, max=limit).astype(kind)


def setup_inputs(seed: int = 0) -> dict:
    keys = jax.random.split(jax.random.key(seed), 11)
    query_rows = gaussian(keys[0], (SEQS, LENGTH, HEADS * HEAD_DIM), 1.5, 8.0, ((0, 2), (1, 32), (2, 4)))
    key_rows = gaussian(keys[1], (SEQS, LENGTH, KV_HEADS * HEAD_DIM), 1.5, 8.0, ((0, 2), (1, 32), (2, 4)))
    value_rows = gaussian(keys[2], (SEQS, LENGTH, KV_HEADS * HEAD_DIM), 1.0, 6.0, ((0, 2), (1, 32), (2, 4)))
    attention_out = gaussian(keys[3], (SEQS, LENGTH, HEADS * HEAD_DIM), 1.0, 6.0, ((0, 2), (1, 32), (2, 4)))
    output_grad = gaussian(keys[4], (SEQS, LENGTH, HEADS * HEAD_DIM), 4.0, 24.0, ((0, 2), (1, 32), (2, 4)))
    log_norms = draw_log_norms(jax.random.fold_in(keys[10], 71), 0)
    moe_grad = gaussian(keys[6], (SEQS, LENGTH, D), 1.0, 6.0, ((0, 2), (1, 32), (2, 4)))
    expert_ids_keys = jax.random.split(jax.random.fold_in(keys[7], 1), SEQS * LENGTH // TOK_DEV)
    expert_ids_turns = jax.random.permutation(jax.random.fold_in(keys[7], 3), SEQS * LENGTH // TOK_DEV)
    expert_ids = jax.vmap(lambda own, number: deal_out(jax.random.fold_in(keys[7], 2), own, number, TOK_DEV, EXPERTS, TOP, CAP, 2))(expert_ids_keys, expert_ids_turns).reshape((SEQS, LENGTH, TOP))
    route_weight = plant(jax.random.randint(keys[8], (SEQS, LENGTH, TOP), 1, 32768), jax.random.fold_in(keys[8], 1), 1, 32767).astype(jnp.int32)
    hidden_act = gaussian(keys[9], (SEQS, SLOTS, F_ALL), 0.03, 0.1875, ((0, 2), (1, 4), (2, 32)))
    return dict(query_rows=query_rows, key_rows=key_rows, value_rows=value_rows, attention_out=attention_out, output_grad=output_grad, log_norms=log_norms, moe_grad=moe_grad, expert_ids=expert_ids, route_weight=route_weight, hidden_act=hidden_act)


ACCURATE = lax.Precision.HIGHEST

def group_grads(query_g, key_g, value_g, out_g, grad_g, norms_g):
    scale_factor = HEAD_DIM ** (-0.5)
    positions = jnp.arange(LENGTH, dtype=jnp.int32)
    causal = positions[:, None] >= positions[None, :]
    keys_f = key_g.astype(jnp.float32)
    values_f = value_g.astype(jnp.float32)
    key_acc = jnp.zeros(key_g.shape, jnp.float32)
    value_acc = jnp.zeros(value_g.shape, jnp.float32)
    query_parts = []
    for member in range(HEADS // KV_HEADS):
        query_f = query_g[:, :, member].astype(jnp.float32)
        grad_f = grad_g[:, :, member].astype(jnp.float32)
        row_delta = lax.optimization_barrier(jnp.sum(grad_f * out_g[:, :, member].astype(jnp.float32), axis=-1))
        scores = jnp.einsum('sid,sjd->sij', query_f, keys_f, precision=ACCURATE) * scale_factor
        exp_scores = jnp.where(causal[None], jnp.exp(scores - norms_g[:, :, member][:, :, None]), 0.0)
        probability = exp_scores.astype(jnp.bfloat16)
        prob_grad = jnp.einsum('sid,sjd->sij', grad_f, values_f, precision=ACCURATE)
        score_grad = (scale_factor * exp_scores * (prob_grad - row_delta[:, :, None])).astype(jnp.bfloat16)
        score_f = score_grad.astype(jnp.float32)
        query_parts.append(jnp.einsum('sij,sjd->sid', score_f, keys_f, precision=ACCURATE).astype(jnp.bfloat16))
        key_acc = key_acc + jnp.einsum('sij,sid->sjd', score_f, query_f, precision=ACCURATE)
        value_acc = value_acc + jnp.einsum('sij,sid->sjd', probability.astype(jnp.float32), grad_f, precision=ACCURATE)
    return (jnp.stack(query_parts, axis=2), key_acc.astype(jnp.bfloat16), value_acc.astype(jnp.bfloat16))

def reference(query_rows, key_rows, value_rows, attention_out, output_grad, log_norms, moe_grad, expert_ids, route_weight, hidden_act):
    members = HEADS // KV_HEADS

    def split_heads(array):
        return jnp.moveaxis(array.reshape(SEQS, LENGTH, KV_HEADS, members, HEAD_DIM), 2, 0)

    def split_kv(array):
        return jnp.moveaxis(array.reshape(SEQS, LENGTH, KV_HEADS, HEAD_DIM), 2, 0)
    norms = jnp.moveaxis(log_norms.reshape(SEQS, LENGTH, KV_HEADS, members), 2, 0)

    def one_group(items):
        return group_grads(items[0], items[1], items[2], items[3], items[4], items[5])
    query_all, key_all, value_all = lax.map(one_group, (split_heads(query_rows), split_kv(key_rows), split_kv(value_rows), split_heads(attention_out), split_heads(output_grad), norms))
    query_grad = jnp.moveaxis(query_all, 0, 2).reshape(SEQS, LENGTH, HEADS * HEAD_DIM)
    key_grad = jnp.moveaxis(key_all, 0, 2).reshape(SEQS, LENGTH, KV_HEADS * HEAD_DIM)
    value_grad = jnp.moveaxis(value_all, 0, 2).reshape(SEQS, LENGTH, KV_HEADS * HEAD_DIM)
    chosen_ids = expert_ids.reshape(SEQS, N_CP, TOK_DEV, TOP)
    weights_real = route_weight.reshape(SEQS, N_CP, TOK_DEV, TOP).astype(jnp.float32) / 32768.0
    grad_rows = moe_grad.reshape(SEQS, N_CP, TOK_DEV, D).astype(jnp.float32)
    slot_axis = jnp.arange(CAP, dtype=jnp.int32)

    def expert_grad(expert):
        chosen = chosen_ids == expert
        route_hits = lax.optimization_barrier(jnp.sum(chosen.astype(jnp.int32), axis=-1))
        slot_rank = jnp.cumsum(route_hits, axis=2) - route_hits
        route_scale = lax.optimization_barrier(jnp.sum(jnp.where(chosen, weights_real, 0.0), axis=-1))
        placed = (slot_rank[..., None] == slot_axis) & (route_hits[..., None] > 0)
        combine = jnp.where(placed, route_scale[..., None], 0.0)
        routed = jnp.einsum('sctk,sctd->sckd', combine, grad_rows, precision=ACCURATE).astype(jnp.bfloat16)
        hidden_block = lax.dynamic_slice_in_dim(hidden_act, (expert * F).astype(jnp.int32), F, 2)
        return jnp.dot(hidden_block.reshape(SEQS * SLOTS, F).T, routed.reshape(SEQS * SLOTS, D), preferred_element_type=jnp.float32).astype(jnp.bfloat16)
    down_grad = lax.map(expert_grad, jnp.arange(EXPERTS, dtype=jnp.int32)).reshape(F_ALL, D)
    return (query_grad, key_grad, value_grad, down_grad)
```

```python
import functools

import jax
import jax.numpy as jnp
from jax import lax
from jax.experimental import pallas as pl
from jax.experimental.pallas import tpu as pltpu
from jax.sharding import Mesh, PartitionSpec as P

HEAD_DIM = 128
MEMBERS = 6
EXPERTS = 8
CAPACITY = 48
TOKENS = 128
SCALE = HEAD_DIM ** (-0.5)
LOG2E = 1.4426950408889634
SWAP = [(0, 1), (1, 0)]
RIGHT = [(i, (i + 1) % 4) for i in range(4)]
LEFT = [(i, (i - 1) % 4) for i in range(4)]
Z = ("zq", "zl")
HALF = MEMBERS * HEAD_DIM
F32 = jnp.float32
BF16 = jnp.bfloat16


def vmem_specs(count):
    return [pl.BlockSpec(memory_space=pltpu.VMEM)] * count


def mxu(a, b, contract=((1,), (0,))):
    return lax.dot_general(a, b, (contract, ((), ())), preferred_element_type=F32)


def route_kernel(ids_ref, codes_ref, grad_ref, out_ref):
    expert = lax.broadcasted_iota(jnp.int32, (EXPERTS, TOKENS), 0)
    first = expert == ids_ref[0:1, :]
    second = expert == ids_ref[1:2, :]
    real = codes_ref[...].astype(F32) * (1.0 / 32768.0)
    hits = jnp.where(first, 1.0, 0.0) + jnp.where(second, 1.0, 0.0)
    scale = jnp.where(first, real[0:1, :], 0.0) + jnp.where(second, real[1:2, :], 0.0)
    earlier = lax.broadcasted_iota(jnp.int32, (TOKENS, TOKENS), 0)
    later = lax.broadcasted_iota(jnp.int32, (TOKENS, TOKENS), 1)
    before = jnp.where(earlier < later, 1.0, 0.0).astype(BF16)
    rank = mxu(hits.astype(BF16), before)
    rank = jnp.where(hits > 0.0, rank, -1.0)
    slot = lax.broadcasted_iota(jnp.int32, (CAPACITY, TOKENS), 0).astype(F32)
    grads = grad_ref[...]
    for e in range(EXPERTS):
        placed = rank[e : e + 1, :] == slot
        picked = mxu(jnp.where(placed, 1.0, 0.0).astype(BF16), grads)
        weight = jnp.sum(jnp.where(placed, scale[e : e + 1, :], 0.0), axis=1, keepdims=True)
        out_ref[e] = (picked * weight).astype(BF16)


def route(ids, codes, grads):
    return pl.pallas_call(
        route_kernel,
        out_shape=jax.ShapeDtypeStruct((EXPERTS, CAPACITY, grads.shape[1]), BF16),
        in_specs=vmem_specs(3),
        out_specs=vmem_specs(1)[0],
        compiler_params=pltpu.CompilerParams(vmem_limit_bytes=32 << 20),
        name="route",
    )(ids, codes, grads)


def pack_kernel(
    place_ref, query_ref, grad_ref, out_ref, norms_ref, keep_ref, send_ref, keep_rows_ref,
    send_rows_ref, delta_ref,
):
    xh = place_ref[0]
    for head in range(2 * MEMBERS):
        columns = slice(head * HEAD_DIM, (head + 1) * HEAD_DIM)
        product = grad_ref[:, columns].astype(F32) * out_ref[:, columns].astype(F32)
        delta_ref[head // MEMBERS, head % MEMBERS : head % MEMBERS + 1, :] = jnp.sum(
            product.T, axis=0, keepdims=True
        )
    for side, pack_ref, rows_ref in ((xh, keep_ref, keep_rows_ref), (1 - xh, send_ref, send_rows_ref)):
        columns = pl.ds(pl.multiple_of(side * HALF, HEAD_DIM), HALF)
        pack_ref[:, 0:HALF] = query_ref[:, columns]
        pack_ref[:, HALF : 2 * HALF] = grad_ref[:, columns]
        rows_ref[0:8, :] = norms_ref[side] * LOG2E
        rows_ref[8:16, :] = delta_ref[side]


def pack(xh, query, grad, out, norms):
    width = query.shape[1]
    shape = jax.ShapeDtypeStruct((TOKENS, width), BF16)
    rows = jax.ShapeDtypeStruct((16, TOKENS), F32)
    return pl.pallas_call(
        pack_kernel,
        out_shape=(shape, shape, rows, rows),
        in_specs=[pl.BlockSpec(memory_space=pltpu.SMEM)] + vmem_specs(4),
        out_specs=tuple(vmem_specs(4)),
        scratch_shapes=[pltpu.VMEM((2, 8, TOKENS), F32)],
        compiler_params=pltpu.CompilerParams(vmem_limit_bytes=32 << 20),
        name="pack",
    )(xh[None], query, grad, out, norms)


def attention_kernel(
    place_ref, kv_ref, p00, p01, p10, p11, r00, r01, r10, r11,
    dkv_ref, keep_ref, send_ref,
    q_ref, do_ref, qt_ref, dot_ref, dqt_ref, rows_ref, diff_ref, acc_ref,
):
    xh, z, co = place_ref[0], place_ref[1], place_ref[2]
    packs = ((p00, p01), (p10, p11))
    rows = ((r00, r01), (r10, r11))
    for g in range(2):
        for c in range(2):
            span = slice(c * TOKENS, (c + 1) * TOKENS)
            rows_ref[g, :, span] = rows[g][c][...]
            for h in range(MEMBERS):
                block = packs[g][c][:, h * HEAD_DIM : (h + 1) * HEAD_DIM]
                q_ref[g, h, span, :] = block
                qt_ref[g, h, :, span] = block.T
                block = packs[g][c][:, HALF + h * HEAD_DIM : HALF + (h + 1) * HEAD_DIM]
                do_ref[g, h, span, :] = block
                dot_ref[g, h, :, span] = block.T
    dqt_ref[...] = jnp.zeros_like(dqt_ref)
    key_row = lax.broadcasted_iota(jnp.int32, (256, 256), 0)
    query_row = lax.broadcasted_iota(jnp.int32, (256, 256), 1)
    own = query_row < TOKENS
    query_at = jnp.where(own, query_row + co * TOKENS, query_row - TOKENS + (1 - co) * TOKENS)
    diff_ref[...] = query_at - jnp.where(key_row < TOKENS, key_row, key_row + TOKENS)

    def chunk(index, _):
        slot, t = index // 4, index % 4
        xh_key = jnp.where(slot == 0, xh, 1 - xh)
        kv = kv_ref[pl.ds(2 * t, 2), slot].reshape(256, 256)
        key, value = kv[:, :HEAD_DIM], kv[:, HEAD_DIM:]
        key_t = key.T
        acc_ref[...] = jnp.zeros_like(acc_ref)
        for g in range(2):
            xh_query = xh if g == 0 else 1 - xh
            seen = (xh_key < xh_query) | ((xh_key == xh_query) & (t <= z // 2))
            bound = (xh_key - xh_query) * 2048 + t * 512 + co * TOKENS - z * 256

            @pl.when(seen)
            def _():
                key_part = jnp.zeros((256, HEAD_DIM), F32)
                value_part = jnp.zeros((256, HEAD_DIM), F32)
                for h in range(MEMBERS):
                    scores = mxu(key, qt_ref[g, h])
                    exp_scores = jnp.exp2(scores * (SCALE * LOG2E) - rows_ref[g, h : h + 1, :])
                    exp_scores = jnp.where(diff_ref[...] >= bound, exp_scores, 0.0)
                    prob_grad = mxu(value, dot_ref[g, h])
                    value_part += mxu(exp_scores.astype(BF16), do_ref[g, h])
                    score_grad = (
                        (SCALE * exp_scores) * (prob_grad - rows_ref[g, 8 + h : 9 + h, :])
                    ).astype(BF16)
                    key_part += mxu(score_grad, q_ref[g, h])
                    dqt_ref[g, h] += mxu(key_t, score_grad)
                acc_ref[:, :HEAD_DIM] += key_part
                acc_ref[:, HEAD_DIM:] += value_part

        dkv_ref[pl.ds(2 * t, 2), slot] = acc_ref[...].astype(BF16).reshape(2, TOKENS, 256)
        return 0

    lax.fori_loop(0, 8, chunk, 0)
    for g in range(2):
        for h in range(MEMBERS):
            columns = slice(h * HEAD_DIM, (h + 1) * HEAD_DIM)
            total = dqt_ref[g, h]
            keep_ref[g, :, columns] = total[:, :TOKENS].T
            send_ref[g, :, columns] = total[:, TOKENS:].T.astype(BF16)


def attention(place, kv, packs, rows):
    return pl.pallas_call(
        attention_kernel,
        out_shape=(
            jax.ShapeDtypeStruct(kv.shape, BF16),
            jax.ShapeDtypeStruct((2, TOKENS, HALF), F32),
            jax.ShapeDtypeStruct((2, TOKENS, HALF), BF16),
        ),
        in_specs=[pl.BlockSpec(memory_space=pltpu.SMEM)] + vmem_specs(9),
        out_specs=tuple(vmem_specs(3)),
        scratch_shapes=[
            pltpu.VMEM((2, MEMBERS, 256, HEAD_DIM), BF16),
            pltpu.VMEM((2, MEMBERS, 256, HEAD_DIM), BF16),
            pltpu.VMEM((2, MEMBERS, HEAD_DIM, 256), BF16),
            pltpu.VMEM((2, MEMBERS, HEAD_DIM, 256), BF16),
            pltpu.VMEM((2, MEMBERS, HEAD_DIM, 256), F32),
            pltpu.VMEM((2, 16, 256), F32),
            pltpu.VMEM((256, 256), jnp.int32),
            pltpu.VMEM((256, 256), F32),
        ],
        compiler_params=pltpu.CompilerParams(vmem_limit_bytes=48 << 20),
        name="attention",
    )(place, kv, *packs, *rows)


def down_kernel(place_ref, *refs):
    routed = refs[0:4]
    hidden = refs[4:14]
    out_ref, gathered_ref = refs[14], refs[15]
    dp, tp = place_ref[0], place_ref[1]

    @pl.when(pl.program_id(0) == 0)
    def _():
        for s in range(2):
            seq = dp if s == 0 else 1 - dp
            own, left, right, far_low, far_high = hidden[5 * s : 5 * s + 5]
            here = seq * 4 + tp
            before = seq * 4 + lax.rem(tp + 3, 4)
            after = seq * 4 + lax.rem(tp + 1, 4)
            far = seq * 4 + lax.rem(tp + 2, 4)
            for m in range(4):
                gathered_ref[m, here] = own[m]
                gathered_ref[m, before] = left[m]
                gathered_ref[m, after] = right[m]
                gathered_ref[m, far] = far_low[m] if m < 2 else far_high[m - 2]

    total = None
    for m in range(4):
        left = gathered_ref[m].reshape(768, gathered_ref.shape[3])
        right = routed[m][...].reshape(768, out_ref.shape[1])
        part = mxu(left, right, ((0,), (0,)))
        total = part if total is None else total + part
    out_ref[...] = total.astype(BF16)


def down(place, routed, hidden, tile=512):
    width = routed.shape[-1]
    rows = hidden[0].shape[-1]
    whole = lambda i, p: (0, 0, 0)
    return pl.pallas_call(
        down_kernel,
        grid_spec=pltpu.PrefetchScalarGridSpec(
            num_scalar_prefetch=1,
            grid=(width // tile,),
            in_specs=[
                pl.BlockSpec((None, 8, 96, tile), functools.partial(lambda m, i, p: (m, 0, 0, i), m))
                for m in range(4)
            ]
            + [pl.BlockSpec(h.shape, whole, pipeline_mode=pl.Buffered(1)) for h in hidden],
            out_specs=pl.BlockSpec((rows, tile), lambda i, p: (0, i)),
            scratch_shapes=[pltpu.VMEM((4, 8, 96, rows), BF16)],
        ),
        out_shape=jax.ShapeDtypeStruct((rows, width), BF16),
        compiler_params=pltpu.CompilerParams(vmem_limit_bytes=56 << 20),
        name="down",
    )(place, routed, routed, routed, routed, *hidden)


def local(
    query_rows,
    key_rows,
    value_rows,
    attention_out,
    output_grad,
    log_norms,
    moe_grad,
    expert_ids,
    route_weight,
    hidden_act,
):
    xh, co, dp, tp = (lax.axis_index(name) for name in ("xh", "co", "dp", "tp"))
    z = lax.axis_index(Z)

    def by_side(array, side):
        return lax.dynamic_index_in_dim(array, side, 0, keepdims=False)

    kv = jnp.concatenate(
        [key_rows[0].reshape(TOKENS, 2, HEAD_DIM), value_rows[0].reshape(TOKENS, 2, HEAD_DIM)],
        axis=2,
    ).transpose(1, 0, 2)
    kv_other = lax.ppermute(by_side(kv, 1 - xh), "xh", SWAP)
    kv_all = lax.all_gather(jnp.stack([by_side(kv, xh), kv_other]), Z, axis=0)

    hidden = hidden_act[0].reshape(2, 4, CAPACITY, 2, 1024).transpose(3, 1, 0, 2, 4)
    hidden = hidden.reshape(2, 4, 2 * CAPACITY, 1024)
    hidden_own = by_side(hidden, dp)
    hidden_other = lax.ppermute(by_side(hidden, 1 - dp), "dp", SWAP)

    routed = route(expert_ids[0].T, route_weight[0].T, moe_grad[0])
    arrived = lax.all_to_all(routed, ("xh", "zq"), 0, 0, tiled=True)
    arrived = lax.all_gather(arrived, ("zl", "co", "dp"), axis=0)
    arrived = arrived.reshape(4, 8, 2 * CAPACITY, moe_grad.shape[2])

    pieces = []
    for piece in (hidden_own, hidden_other):
        left = lax.ppermute(piece, "tp", RIGHT)
        right = lax.ppermute(piece, "tp", LEFT)
        far_low = lax.ppermute(left[:2], "tp", RIGHT)
        far_high = lax.ppermute(right[2:], "tp", LEFT)
        pieces += [piece, left, right, far_low, far_high]

    norms = jnp.pad(log_norms[0].T.reshape(2, MEMBERS, TOKENS), ((0, 0), (0, 2), (0, 0)))
    keep, send, keep_rows, send_rows = pack(
        xh, query_rows[0], output_grad[0], attention_out[0], norms
    )
    across = lax.ppermute(send, "xh", SWAP)
    across_rows = lax.ppermute(send_rows, "xh", SWAP)
    packs = (keep, lax.ppermute(keep, "co", SWAP), across, lax.ppermute(across, "co", SWAP))
    rows_near = lax.ppermute(jnp.stack([keep_rows, across_rows]), "co", SWAP)
    rows = (keep_rows, rows_near[0], across_rows, rows_near[1])
    dkv, dq_keep, dq_send = attention(jnp.stack([xh, z, co]), kv_all, packs, rows)

    dq = (dq_keep + lax.ppermute(dq_send, "co", SWAP).astype(F32)).astype(BF16)
    dq_across = lax.ppermute(dq[1], "xh", SWAP)
    dkv = jnp.sum(lax.all_to_all(dkv, Z, 0, 0, tiled=True).astype(F32), axis=0).astype(BF16)
    dkv_across = lax.ppermute(dkv[1], "xh", SWAP)

    def in_order(mine, other):
        low = jnp.where(xh == 0, mine, other)
        high = jnp.where(xh == 0, other, mine)
        return low, high

    query_grad = jnp.concatenate(in_order(dq[0], dq_across), axis=1)[None]
    low, high = in_order(dkv[0], dkv_across)
    key_grad = jnp.concatenate([low[:, :HEAD_DIM], high[:, :HEAD_DIM]], axis=1)[None]
    value_grad = jnp.concatenate([low[:, HEAD_DIM:], high[:, HEAD_DIM:]], axis=1)[None]
    down_grad = down(jnp.stack([dp, tp]), arrived, pieces)
    return (query_grad, key_grad, value_grad, down_grad)


def solution(mesh):
    fine = Mesh(mesh.devices.reshape(2, 4, 2, 2, 4, 2), ("xh", "zq", "zl", "co", "tp", "dp"))
    cp = ("xh", "zq", "zl", "co")
    return jax.shard_map(
        local,
        mesh=fine,
        in_specs=(
            P("dp", cp, "tp"),
            P("dp", cp, "tp"),
            P("dp", cp, "tp"),
            P("dp", cp, "tp"),
            P("dp", cp, "tp"),
            P("dp", cp, "tp"),
            P("dp", cp, "tp"),
            P("dp", cp, None),
            P("dp", cp, None),
            P("dp", "tp", cp),
        ),
        out_specs=(
            P("dp", cp, "tp"),
            P("dp", cp, "tp"),
            P("dp", cp, "tp"),
            P(cp + ("dp",), "tp"),
        ),
        check_vma=False,
    )
```

```python
import functools

import jax
import jax.numpy as jnp
from jax import lax
from jax.experimental import pallas as pl
from jax.experimental.pallas import tpu as pltpu
from jax.sharding import Mesh, PartitionSpec as P

HEAD_DIM = 128
MEMBERS = 6
EXPERTS = 8
CAPACITY = 48
TOKENS = 128
SCALE = HEAD_DIM ** (-0.5)
LOG2E = 1.4426950408889634
SWAP = [(0, 1), (1, 0)]
RIGHT = [(i, (i + 1) % 4) for i in range(4)]
LEFT = [(i, (i - 1) % 4) for i in range(4)]
ACROSS = [(i, (i + 2) % 4) for i in range(4)]
Z = ("zq", "zl")
HALF = MEMBERS * HEAD_DIM
F32 = jnp.float32
BF16 = jnp.bfloat16


def vmem_specs(count):
    return [pl.BlockSpec(memory_space=pltpu.VMEM)] * count


def mxu(a, b, contract=((1,), (0,))):
    return lax.dot_general(a, b, (contract, ((), ())), preferred_element_type=F32)


def route_kernel(ids_ref, codes_ref, grad_ref, _, out_ref):
    expert = lax.broadcasted_iota(jnp.int32, (EXPERTS, TOKENS), 0)
    first = expert == ids_ref[0:1, :]
    second = expert == ids_ref[1:2, :]
    real = codes_ref[...].astype(F32) * (1.0 / 32768.0)
    hits = jnp.where(first, 1.0, 0.0) + jnp.where(second, 1.0, 0.0)
    scale = jnp.where(first, real[0:1, :], 0.0) + jnp.where(second, real[1:2, :], 0.0)
    earlier = lax.broadcasted_iota(jnp.int32, (TOKENS, TOKENS), 0)
    later = lax.broadcasted_iota(jnp.int32, (TOKENS, TOKENS), 1)
    before = jnp.where(earlier < later, 1.0, 0.0).astype(BF16)
    rank = mxu(hits.astype(BF16), before)
    rank = jnp.where(hits > 0.0, rank, -1.0)
    slot = lax.broadcasted_iota(jnp.int32, (CAPACITY, TOKENS), 0).astype(F32)
    grads = grad_ref[...]
    for e in range(EXPERTS):
        placed = rank[e : e + 1, :] == slot
        picked = mxu(jnp.where(placed, 1.0, 0.0).astype(BF16), grads)
        weight = jnp.sum(jnp.where(placed, scale[e : e + 1, :], 0.0), axis=1, keepdims=True)
        out_ref[e] = (picked * weight).astype(BF16)


def route(ids, codes, grads, after):
    return pl.pallas_call(
        route_kernel,
        out_shape=jax.ShapeDtypeStruct((EXPERTS, CAPACITY, grads.shape[1]), BF16),
        in_specs=vmem_specs(4),
        out_specs=vmem_specs(1)[0],
        compiler_params=pltpu.CompilerParams(vmem_limit_bytes=32 << 20),
        name="route",
    )(ids, codes, grads, after)


def pair_kernel(place_ref, key_ref, value_ref, keep_ref, send_ref):
    xh = place_ref[0]
    for side, out_ref in ((xh, keep_ref), (1 - xh, send_ref)):
        columns = pl.ds(pl.multiple_of(side * HEAD_DIM, HEAD_DIM), HEAD_DIM)
        out_ref[:, 0:HEAD_DIM] = key_ref[:, columns]
        out_ref[:, HEAD_DIM:] = value_ref[:, columns]


def pair(xh, key, value):
    shape = jax.ShapeDtypeStruct(key.shape, BF16)
    return pl.pallas_call(
        pair_kernel,
        out_shape=(shape, shape),
        in_specs=[pl.BlockSpec(memory_space=pltpu.SMEM)] + vmem_specs(2),
        out_specs=tuple(vmem_specs(2)),
        name="pair",
    )(xh[None], key, value)


def halves_kernel(place_ref, hidden_ref, _, keep_ref, send_ref):
    dp = place_ref[0]
    for side, out_ref in ((dp, keep_ref), (1 - dp, send_ref)):
        columns = pl.ds(pl.multiple_of(side * 1024, 1024), 1024)
        for part in range(2):
            rows = slice(part * CAPACITY, (part + 1) * CAPACITY)
            out_ref[0, rows, :] = hidden_ref[part, 0, :, columns]


def halves(dp, hidden, after):
    shape = jax.ShapeDtypeStruct((4, 2 * CAPACITY, 1024), BF16)
    block = pl.BlockSpec((1, 2 * CAPACITY, 1024), lambda m: (m, 0, 0))
    return pl.pallas_call(
        halves_kernel,
        grid=(4,),
        out_shape=(shape, shape),
        in_specs=[
            pl.BlockSpec(memory_space=pltpu.SMEM),
            pl.BlockSpec((2, 1, CAPACITY, 2048), lambda m: (0, m, 0, 0)),
            pl.BlockSpec(memory_space=pl.ANY),
        ],
        out_specs=(block, block),
        name="halves",
    )(dp[None], hidden, after)


def pack_kernel(
    place_ref, query_ref, grad_ref, out_ref, norms_ref, _, keep_ref, send_ref, token_ref, delta_ref
):
    token_ref[...] = jnp.zeros_like(token_ref)
    xh = place_ref[0]
    for head in range(2 * MEMBERS):
        columns = slice(head * HEAD_DIM, (head + 1) * HEAD_DIM)
        product = grad_ref[:, columns].astype(F32) * out_ref[:, columns].astype(F32)
        delta_ref[head // MEMBERS, head % MEMBERS : head % MEMBERS + 1, :] = jnp.sum(
            product.T, axis=0, keepdims=True
        )
    for side, pack_ref in ((xh, keep_ref), (1 - xh, send_ref)):
        columns = pl.ds(pl.multiple_of(side * HALF, HEAD_DIM), HALF)
        pack_ref[0:TOKENS, 0:HALF] = query_ref[:, columns]
        pack_ref[0:TOKENS, HALF : 2 * HALF] = grad_ref[:, columns]
        rest = jnp.concatenate([norms_ref[side] * LOG2E, delta_ref[side]], axis=0)
        pack_ref[TOKENS : TOKENS + 16, :] = jnp.zeros((16, 2 * HALF), BF16)
        for term in range(3):
            part = rest.astype(BF16)
            pack_ref[TOKENS : TOKENS + 16, term * TOKENS : (term + 1) * TOKENS] = part
            rest = rest - part.astype(F32)


def pack(xh, query, grad, out, norms, after):
    shape = jax.ShapeDtypeStruct((TOKENS + 16, query.shape[1]), BF16)
    return pl.pallas_call(
        pack_kernel,
        out_shape=(shape, shape, jax.ShapeDtypeStruct((8, HEAD_DIM), F32)),
        in_specs=[pl.BlockSpec(memory_space=pltpu.SMEM)]
        + vmem_specs(4)
        + [pl.BlockSpec(memory_space=pl.ANY)],
        out_specs=tuple(vmem_specs(3)),
        scratch_shapes=[pltpu.VMEM((2, 8, TOKENS), F32)],
        compiler_params=pltpu.CompilerParams(vmem_limit_bytes=32 << 20),
        name="pack",
    )(xh[None], query, grad, out, norms, after)


def attention_kernel(
    place_ref, kv_ref, p00, p01, p10, p11, *refs
):
    dkv_ref, keep_ref, send_ref = refs[-11:-8]
    q_ref, do_ref, qt_ref, dot_ref, dqt_ref, rows_ref, diff_ref, acc_ref = refs[-8:]
    xh, z, co = place_ref[0], place_ref[1], place_ref[2]
    packs = ((p00, p01), (p10, p11))
    for g in range(2):
        for c in range(2):
            span = slice(c * TOKENS, (c + 1) * TOKENS)
            terms = packs[g][c][TOKENS : TOKENS + 16, 0 : 3 * TOKENS].astype(F32)
            rows_ref[g, :, span] = (
                terms[:, 0:TOKENS] + terms[:, TOKENS : 2 * TOKENS] + terms[:, 2 * TOKENS :]
            )
            for h in range(MEMBERS):
                block = packs[g][c][:TOKENS, h * HEAD_DIM : (h + 1) * HEAD_DIM]
                q_ref[g, h, span, :] = block
                qt_ref[g, h, :, span] = block.T
                block = packs[g][c][:TOKENS, HALF + h * HEAD_DIM : HALF + (h + 1) * HEAD_DIM]
                do_ref[g, h, span, :] = block
                dot_ref[g, h, :, span] = block.T
    dqt_ref[...] = jnp.zeros_like(dqt_ref)
    key_row = lax.broadcasted_iota(jnp.int32, (256, 256), 0)
    query_row = lax.broadcasted_iota(jnp.int32, (256, 256), 1)
    own = query_row < TOKENS
    query_at = jnp.where(own, query_row + co * TOKENS, query_row - TOKENS + (1 - co) * TOKENS)
    diff_ref[...] = query_at - jnp.where(key_row < TOKENS, key_row, key_row + TOKENS)

    def chunk(index, _):
        slot, t = index // 4, index % 4
        xh_key = jnp.where(slot == 0, xh, 1 - xh)
        kv = kv_ref[pl.ds(2 * t, 2), slot].reshape(256, 256)
        key, value = kv[:, :HEAD_DIM], kv[:, HEAD_DIM:]
        key_t = key.T
        acc_ref[...] = jnp.zeros_like(acc_ref)
        for g in range(2):
            xh_query = xh if g == 0 else 1 - xh
            seen = (xh_key < xh_query) | ((xh_key == xh_query) & (t <= z // 2))
            bound = (xh_key - xh_query) * 2048 + t * 512 + co * TOKENS - z * 256

            @pl.when(seen)
            def _():
                key_part = jnp.zeros((256, HEAD_DIM), F32)
                value_part = jnp.zeros((256, HEAD_DIM), F32)
                for h in range(MEMBERS):
                    scores = mxu(key, qt_ref[g, h])
                    exp_scores = jnp.exp2(scores * (SCALE * LOG2E) - rows_ref[g, h : h + 1, :])
                    exp_scores = jnp.where(diff_ref[...] >= bound, exp_scores, 0.0)
                    prob_grad = mxu(value, dot_ref[g, h])
                    value_part += mxu(exp_scores.astype(BF16), do_ref[g, h])
                    score_grad = (
                        (SCALE * exp_scores) * (prob_grad - rows_ref[g, 8 + h : 9 + h, :])
                    ).astype(BF16)
                    key_part += mxu(score_grad, q_ref[g, h])
                    dqt_ref[g, h] += mxu(key_t, score_grad)
                acc_ref[:, :HEAD_DIM] += key_part
                acc_ref[:, HEAD_DIM:] += value_part

        dkv_ref[pl.ds(2 * t, 2), slot] = acc_ref[...].astype(BF16).reshape(2, TOKENS, 256)
        return 0

    lax.fori_loop(0, 8, chunk, 0)
    for g in range(2):
        for h in range(MEMBERS):
            columns = slice(h * HEAD_DIM, (h + 1) * HEAD_DIM)
            total = dqt_ref[g, h]
            keep_ref[g, :, columns] = total[:, :TOKENS].T
            send_ref[g, :, columns] = total[:, TOKENS:].T.astype(BF16)


def attention(place, kv, packs, after):
    return pl.pallas_call(
        attention_kernel,
        out_shape=(
            jax.ShapeDtypeStruct((8, 2, TOKENS, 256), BF16),
            jax.ShapeDtypeStruct((2, TOKENS, HALF), F32),
            jax.ShapeDtypeStruct((2, TOKENS, HALF), BF16),
        ),
        in_specs=[pl.BlockSpec(memory_space=pltpu.SMEM)]
        + vmem_specs(5)
        + [pl.BlockSpec(memory_space=pl.ANY)] * len(after),
        out_specs=tuple(vmem_specs(3)),
        scratch_shapes=[
            pltpu.VMEM((2, MEMBERS, 256, HEAD_DIM), BF16),
            pltpu.VMEM((2, MEMBERS, 256, HEAD_DIM), BF16),
            pltpu.VMEM((2, MEMBERS, HEAD_DIM, 256), BF16),
            pltpu.VMEM((2, MEMBERS, HEAD_DIM, 256), BF16),
            pltpu.VMEM((2, MEMBERS, HEAD_DIM, 256), F32),
            pltpu.VMEM((2, 16, 256), F32),
            pltpu.VMEM((256, 256), jnp.int32),
            pltpu.VMEM((256, 256), F32),
        ],
        cost_estimate=pl.CostEstimate(
            flops=16_000_000_000, transcendentals=5_000_000, bytes_accessed=8_000_000
        ),
        compiler_params=pltpu.CompilerParams(vmem_limit_bytes=48 << 20),
        name="attention",
    )(place, kv, *packs, *after)


ANY = pl.BlockSpec(memory_space=pl.ANY)
HALF_COST = 6
KV_COST = 10


def joined_kernel(keep_ref, other_ref, out_ref):
    out_ref[0] = keep_ref[...]
    out_ref[1] = other_ref[...]


def joined(keep, other):
    return pl.pallas_call(
        joined_kernel,
        out_shape=jax.ShapeDtypeStruct((2,) + keep.shape, keep.dtype),
        in_specs=vmem_specs(2),
        out_specs=vmem_specs(1)[0],
        name="joined",
    )(keep, other)


def mark_kernel(_, out_ref):
    out_ref[...] = jnp.zeros_like(out_ref)


def mark(after, cost):
    return pl.pallas_call(
        mark_kernel,
        out_shape=jax.ShapeDtypeStruct((8, HEAD_DIM), F32),
        in_specs=[ANY],
        out_specs=vmem_specs(1)[0],
        cost_estimate=pl.CostEstimate(
            flops=cost * 1_000_000_000, transcendentals=0, bytes_accessed=1_000_000
        ),
        name="mark",
    )(after)


def half_kernel(first, rows_ref, out_ref):
    out_ref[...] = rows_ref[first : first + 2]


def half(rows, first, cost=HALF_COST):
    shape = (2,) + rows.shape[1:]
    return pl.pallas_call(
        functools.partial(half_kernel, first),
        out_shape=jax.ShapeDtypeStruct(shape, rows.dtype),
        in_specs=vmem_specs(1),
        out_specs=vmem_specs(1)[0],
        cost_estimate=pl.CostEstimate(
            flops=cost * 1_000_000_000, transcendentals=0, bytes_accessed=2_000_000
        ),
        name="half",
    )(rows)


def down_kernel(shards, place_ref, *refs):
    hidden, (out_ref, gathered_ref) = (refs[-10:-6], refs[-6:-2]), refs[-2:]
    routed = refs[:-10]
    tp, zl, co = (place_ref[i] for i in range(3))

    @pl.when(pl.program_id(0) == 0)
    def _():
        for n, (other_seq, other_z, other_core) in enumerate(shards):
            m = 2 * (1 - zl if other_z else zl) + (1 - co if other_core else co)
            for piece, step in zip(hidden[other_seq], (0, 3, 1, 2)):
                gathered_ref[n, lax.rem(tp + step, 4)] = piece[m]

    left_side = gathered_ref[...].reshape(len(shards) * 384, gathered_ref.shape[3])
    right_side = jnp.concatenate([r[...].reshape(-1, out_ref.shape[1]) for r in routed], axis=0)
    out_ref[...] = mxu(left_side, right_side, ((0,), (0,))).astype(BF16)


def down(place, shards, routed, hidden, tile=512):
    width = routed[0].shape[-1]
    rows = hidden[0].shape[-1]
    whole = pl.BlockSpec((4, 96, rows), lambda i, p: (0, 0, 0), pipeline_mode=pl.Buffered(1))
    return pl.pallas_call(
        functools.partial(down_kernel, shards),
        grid_spec=pltpu.PrefetchScalarGridSpec(
            num_scalar_prefetch=1,
            grid=(width // tile,),
            in_specs=[pl.BlockSpec(r.shape[:2] + (tile,), lambda i, p: (0, 0, i)) for r in routed]
            + [whole] * 8,
            out_specs=pl.BlockSpec((rows, tile), lambda i, p: (0, i)),
            scratch_shapes=[pltpu.VMEM((len(shards), 4, 96, rows), BF16)],
        ),
        out_shape=jax.ShapeDtypeStruct((rows, width), BF16),
        cost_estimate=pl.CostEstimate(
            flops=16_000_000_000, transcendentals=0, bytes_accessed=20_000_000
        ),
        compiler_params=pltpu.CompilerParams(vmem_limit_bytes=56 << 20),
        name="down",
    )(place, *routed, *hidden)


def finish_kernel(parts_ref, kept_ref, near_ref, mine_ref, send_ref):
    for side, out_ref in ((0, mine_ref), (1, send_ref)):
        out_ref[:, 0:HALF] = (kept_ref[side] + near_ref[side].astype(F32)).astype(BF16)
        total = parts_ref[0, side].astype(F32)
        for part in range(1, 8):
            total = total + parts_ref[part, side].astype(F32)
        out_ref[:, HALF:] = total.astype(BF16)


def finish(parts, kept, near):
    shape = jax.ShapeDtypeStruct((TOKENS, HALF + 256), BF16)
    return pl.pallas_call(
        finish_kernel,
        out_shape=(shape, shape),
        in_specs=vmem_specs(3),
        out_specs=tuple(vmem_specs(2)),
        compiler_params=pltpu.CompilerParams(vmem_limit_bytes=32 << 20),
        name="finish",
    )(parts, kept, near)


def spread_kernel(place_ref, mine_ref, other_ref, _, query_ref, key_ref, value_ref):
    xh = place_ref[0]
    for side, from_ref in ((xh, mine_ref), (1 - xh, other_ref)):
        wide = pl.ds(pl.multiple_of(side * HALF, HEAD_DIM), HALF)
        narrow = pl.ds(pl.multiple_of(side * HEAD_DIM, HEAD_DIM), HEAD_DIM)
        query_ref[:, wide] = from_ref[:, 0:HALF]
        key_ref[:, narrow] = from_ref[:, HALF : HALF + HEAD_DIM]
        value_ref[:, narrow] = from_ref[:, HALF + HEAD_DIM :]


def spread(xh, mine, other, after):
    shape = lambda width: jax.ShapeDtypeStruct((TOKENS, width), BF16)
    return pl.pallas_call(
        spread_kernel,
        out_shape=(shape(2 * HALF), shape(256), shape(256)),
        in_specs=[pl.BlockSpec(memory_space=pltpu.SMEM)] + vmem_specs(2) + [ANY],
        out_specs=tuple(vmem_specs(3)),
        name="spread",
    )(xh[None], mine, other, after)


def local(
    query_rows,
    key_rows,
    value_rows,
    attention_out,
    output_grad,
    log_norms,
    moe_grad,
    expert_ids,
    route_weight,
    hidden_act,
):
    xh, zl, co, dp, tp = (lax.axis_index(name) for name in ("xh", "zl", "co", "dp", "tp"))
    z = lax.axis_index(Z)

    kv_keep, kv_send = pair(xh, key_rows[0], value_rows[0])
    kv = joined(kv_keep, lax.ppermute(kv_send, "xh", SWAP))
    kv_all = lax.all_gather(kv, Z, axis=0)

    corner = lambda arrays: sum(rows[0, :16, :HEAD_DIM] for rows in arrays)

    norms = jnp.pad(log_norms[0].T.reshape(2, MEMBERS, TOKENS), ((0, 0), (0, 2), (0, 0)))
    keep, send, packed = pack(
        xh, query_rows[0], output_grad[0], attention_out[0], norms, kv_keep
    )
    across = lax.ppermute(send, "xh", SWAP)

    outgoing = route(expert_ids[0].T, route_weight[0].T, moe_grad[0], packed)
    routed = lax.all_to_all(outgoing, ("xh", "zq"), 0, 0, tiled=True)
    routed = routed.reshape(4, 2 * CAPACITY, moe_grad.shape[2])
    by_x = lax.ppermute(routed, "dp", SWAP)
    by_z = lax.ppermute(routed, "zl", SWAP)
    diagonal = (lax.ppermute(half(by_z, 0), "dp", SWAP), lax.ppermute(half(by_x, 2), "zl", SWAP))
    shards = (routed, by_x, by_z) + diagonal
    shards += tuple(lax.ppermute(rows, "co", SWAP) for rows in shards)

    hidden = hidden_act[0].reshape(2, 4, CAPACITY, 2048)
    hidden, hidden_send = halves(dp, hidden, corner([across[None]]) + corner([outgoing]))
    hidden_other = lax.ppermute(hidden_send, "dp", SWAP)
    own = [hidden] + [lax.ppermute(hidden, "tp", move) for move in (RIGHT, LEFT, ACROSS)]
    other = [hidden_other] + [
        lax.ppermute(hidden_other, "tp", move) for move in (RIGHT, LEFT, ACROSS)
    ]

    packs = (keep, lax.ppermute(keep, "co", SWAP), across, lax.ppermute(across, "co", SWAP))
    early = corner([hidden_other] + own[1:])
    dkv, dq_keep, dq_send = attention(
        jnp.stack([xh, z, co]), kv_all, packs, [early, mark(kv_all, KV_COST)]
    )
    dq_near = lax.ppermute(dq_send, "co", SWAP)
    dkv = lax.all_to_all(dkv, Z, 0, 0, tiled=True)
    mine, send = finish(dkv, dq_keep, dq_near)

    names = tuple((seq, z, core) for core in (0, 1) for seq, z in ((0, 0), (1, 0), (0, 1), (1, 1)))
    down_grad = down(jnp.stack([tp, zl, co]), names, shards, own + other)
    grads = spread(xh, mine, lax.ppermute(send, "xh", SWAP), down_grad)
    return tuple(grad[None] for grad in grads) + (down_grad,)


def solution(mesh):
    fine = Mesh(mesh.devices.reshape(2, 4, 2, 2, 4, 2), ("xh", "zq", "zl", "co", "tp", "dp"))
    cp = ("xh", "zq", "zl", "co")
    return jax.shard_map(
        local,
        mesh=fine,
        in_specs=(
            P("dp", cp, "tp"),
            P("dp", cp, "tp"),
            P("dp", cp, "tp"),
            P("dp", cp, "tp"),
            P("dp", cp, "tp"),
            P("dp", cp, "tp"),
            P("dp", cp, "tp"),
            P("dp", cp, None),
            P("dp", cp, None),
            P("dp", "tp", cp),
        ),
        out_specs=(
            P("dp", cp, "tp"),
            P("dp", cp, "tp"),
            P("dp", cp, "tp"),
            P(cp + ("dp",), "tp"),
        ),
        check_vma=False,
    )
```

```python
import functools

import jax
import jax.numpy as jnp
from jax import lax
from jax.experimental import pallas as pl
from jax.experimental.pallas import tpu as pltpu
from jax.sharding import Mesh, PartitionSpec as P

HEAD_DIM = 128
MEMBERS = 6
EXPERTS = 8
CAPACITY = 48
TOKENS = 128
SCALE = HEAD_DIM ** (-0.5)
LOG2E = 1.4426950408889634
SWAP = [(0, 1), (1, 0)]
Z = ("zq", "zl")
HALF = MEMBERS * HEAD_DIM
F32 = jnp.float32
BF16 = jnp.bfloat16


ANY = pl.BlockSpec(memory_space=pl.ANY)


def vmem_specs(count):
    return [pl.BlockSpec(memory_space=pltpu.VMEM)] * count


def mxu(a, b, contract=((1,), (0,))):
    return lax.dot_general(a, b, (contract, ((), ())), preferred_element_type=F32)


def route_kernel(ids_ref, codes_ref, grad_ref, _, out_ref):
    expert = lax.broadcasted_iota(jnp.int32, (EXPERTS, TOKENS), 0)
    first = expert == ids_ref[0:1, :]
    second = expert == ids_ref[1:2, :]
    real = codes_ref[...].astype(F32) * (1.0 / 32768.0)
    hits = jnp.where(first, 1.0, 0.0) + jnp.where(second, 1.0, 0.0)
    scale = jnp.where(first, real[0:1, :], 0.0) + jnp.where(second, real[1:2, :], 0.0)
    earlier = lax.broadcasted_iota(jnp.int32, (TOKENS, TOKENS), 0)
    later = lax.broadcasted_iota(jnp.int32, (TOKENS, TOKENS), 1)
    before = jnp.where(earlier < later, 1.0, 0.0).astype(BF16)
    rank = mxu(hits.astype(BF16), before)
    rank = jnp.where(hits > 0.0, rank, -1.0)
    slot = lax.broadcasted_iota(jnp.int32, (CAPACITY, TOKENS), 0).astype(F32)
    grads = grad_ref[...]
    for e in range(EXPERTS):
        placed = rank[e : e + 1, :] == slot
        picked = mxu(jnp.where(placed, 1.0, 0.0).astype(BF16), grads)
        weight = jnp.sum(jnp.where(placed, scale[e : e + 1, :], 0.0), axis=1, keepdims=True)
        out_ref[e] = (picked * weight).astype(BF16)


def route(ids, codes, grads, after):
    return pl.pallas_call(
        route_kernel,
        out_shape=jax.ShapeDtypeStruct((EXPERTS, CAPACITY, grads.shape[1]), BF16),
        in_specs=vmem_specs(4),
        out_specs=vmem_specs(1)[0],
        compiler_params=pltpu.CompilerParams(vmem_limit_bytes=32 << 20),
        name="route",
    )(ids, codes, grads, after)


def pair_kernel(place_ref, key_ref, value_ref, keep_ref, send_ref):
    xh = place_ref[0]
    for side, out_ref in ((xh, keep_ref), (1 - xh, send_ref)):
        columns = pl.ds(pl.multiple_of(side * HEAD_DIM, HEAD_DIM), HEAD_DIM)
        out_ref[:, 0:HEAD_DIM] = key_ref[:, columns]
        out_ref[:, HEAD_DIM:] = value_ref[:, columns]


def pair(xh, key, value):
    shape = jax.ShapeDtypeStruct(key.shape, BF16)
    return pl.pallas_call(
        pair_kernel,
        out_shape=(shape, shape),
        in_specs=[pl.BlockSpec(memory_space=pltpu.SMEM)] + vmem_specs(2),
        out_specs=tuple(vmem_specs(2)),
        name="pair",
    )(xh[None], key, value)


def halves_kernel(place_ref, hidden_ref, _, keep_ref, send_ref):
    dp = place_ref[0]
    for side, out_ref in ((dp, keep_ref), (1 - dp, send_ref)):
        columns = pl.ds(pl.multiple_of(side * 1024, 1024), 1024)
        for part in range(2):
            rows = slice(part * CAPACITY, (part + 1) * CAPACITY)
            out_ref[0, rows, :] = hidden_ref[part, 0, :, columns]


def halves(dp, hidden, after):
    shape = jax.ShapeDtypeStruct((4, 2 * CAPACITY, 1024), BF16)
    block = pl.BlockSpec((1, 2 * CAPACITY, 1024), lambda m: (m, 0, 0))
    return pl.pallas_call(
        halves_kernel,
        grid=(4,),
        out_shape=(shape, shape),
        in_specs=[
            pl.BlockSpec(memory_space=pltpu.SMEM),
            pl.BlockSpec((2, 1, CAPACITY, 2048), lambda m: (0, m, 0, 0)),
            pl.BlockSpec(memory_space=pl.ANY),
        ],
        out_specs=(block, block),
        name="halves",
    )(dp[None], hidden, after)


def beside_kernel(keep_ref, other_ref, _, out_ref):
    out_ref[0] = keep_ref[...]
    out_ref[1] = other_ref[...]


def beside(keep, other, after):
    block = pl.BlockSpec((1,) + keep.shape[1:], lambda m: (m, 0, 0))
    return pl.pallas_call(
        beside_kernel,
        grid=keep.shape[:1],
        out_shape=jax.ShapeDtypeStruct((2,) + keep.shape, keep.dtype),
        in_specs=[block, block, ANY],
        out_specs=pl.BlockSpec((2, 1) + keep.shape[1:], lambda m: (0, m, 0, 0)),
        name="beside",
    )(keep, other, after)


def pack_kernel(
    place_ref, query_ref, grad_ref, out_ref, norms_ref, _, keep_ref, send_ref, token_ref, delta_ref
):
    token_ref[...] = jnp.zeros_like(token_ref)
    xh = place_ref[0]
    for head in range(2 * MEMBERS):
        columns = slice(head * HEAD_DIM, (head + 1) * HEAD_DIM)
        product = grad_ref[:, columns].astype(F32) * out_ref[:, columns].astype(F32)
        delta_ref[head // MEMBERS, head % MEMBERS : head % MEMBERS + 1, :] = jnp.sum(
            product.T, axis=0, keepdims=True
        )
    for side, pack_ref in ((xh, keep_ref), (1 - xh, send_ref)):
        columns = pl.ds(pl.multiple_of(side * HALF, HEAD_DIM), HALF)
        pack_ref[0:TOKENS, 0:HALF] = query_ref[:, columns]
        pack_ref[0:TOKENS, HALF : 2 * HALF] = grad_ref[:, columns]
        rest = jnp.concatenate([norms_ref[side] * LOG2E, delta_ref[side]], axis=0)
        pack_ref[TOKENS : TOKENS + 16, :] = jnp.zeros((16, 2 * HALF), BF16)
        for term in range(3):
            part = rest.astype(BF16)
            pack_ref[TOKENS : TOKENS + 16, term * TOKENS : (term + 1) * TOKENS] = part
            rest = rest - part.astype(F32)


def pack(xh, query, grad, out, norms, after):
    shape = jax.ShapeDtypeStruct((TOKENS + 16, query.shape[1]), BF16)
    return pl.pallas_call(
        pack_kernel,
        out_shape=(shape, shape, jax.ShapeDtypeStruct((8, HEAD_DIM), F32)),
        in_specs=[pl.BlockSpec(memory_space=pltpu.SMEM)]
        + vmem_specs(4)
        + [pl.BlockSpec(memory_space=pl.ANY)],
        out_specs=tuple(vmem_specs(3)),
        scratch_shapes=[pltpu.VMEM((2, 8, TOKENS), F32)],
        compiler_params=pltpu.CompilerParams(vmem_limit_bytes=32 << 20),
        name="pack",
    )(xh[None], query, grad, out, norms, after)


def attention_kernel(
    place_ref, kv_ref, p00, p01, p10, p11, *refs
):
    dkv_ref, keep_ref, send_ref = refs[-11:-8]
    q_ref, do_ref, qt_ref, dot_ref, dqt_ref, rows_ref, diff_ref, acc_ref = refs[-8:]
    xh, z, co = place_ref[0], place_ref[1], place_ref[2]
    packs = ((p00, p01), (p10, p11))
    for g in range(2):
        for c in range(2):
            span = slice(c * TOKENS, (c + 1) * TOKENS)
            terms = packs[g][c][TOKENS : TOKENS + 16, 0 : 3 * TOKENS].astype(F32)
            rows_ref[g, :, span] = (
                terms[:, 0:TOKENS] + terms[:, TOKENS : 2 * TOKENS] + terms[:, 2 * TOKENS :]
            )
            for h in range(MEMBERS):
                block = packs[g][c][:TOKENS, h * HEAD_DIM : (h + 1) * HEAD_DIM]
                q_ref[g, h, span, :] = block
                qt_ref[g, h, :, span] = block.T
                block = packs[g][c][:TOKENS, HALF + h * HEAD_DIM : HALF + (h + 1) * HEAD_DIM]
                do_ref[g, h, span, :] = block
                dot_ref[g, h, :, span] = block.T
    dqt_ref[...] = jnp.zeros_like(dqt_ref)
    key_row = lax.broadcasted_iota(jnp.int32, (256, 256), 0)
    query_row = lax.broadcasted_iota(jnp.int32, (256, 256), 1)
    own = query_row < TOKENS
    query_at = jnp.where(own, query_row + co * TOKENS, query_row - TOKENS + (1 - co) * TOKENS)
    diff_ref[...] = query_at - jnp.where(key_row < TOKENS, key_row, key_row + TOKENS)

    def chunk(index, _):
        slot, t = index // 4, index % 4
        xh_key = jnp.where(slot == 0, xh, 1 - xh)
        kv = kv_ref[pl.ds(2 * t, 2), slot].reshape(256, 256)
        key, value = kv[:, :HEAD_DIM], kv[:, HEAD_DIM:]
        key_t = key.T
        acc_ref[...] = jnp.zeros_like(acc_ref)
        for g in range(2):
            xh_query = xh if g == 0 else 1 - xh
            seen = (xh_key < xh_query) | ((xh_key == xh_query) & (t <= z // 2))
            bound = (xh_key - xh_query) * 2048 + t * 512 + co * TOKENS - z * 256

            @pl.when(seen)
            def _():
                key_part = jnp.zeros((256, HEAD_DIM), F32)
                value_part = jnp.zeros((256, HEAD_DIM), F32)
                for h in range(MEMBERS):
                    scores = mxu(key, qt_ref[g, h])
                    exp_scores = jnp.exp2(scores * (SCALE * LOG2E) - rows_ref[g, h : h + 1, :])
                    exp_scores = jnp.where(diff_ref[...] >= bound, exp_scores, 0.0)
                    prob_grad = mxu(value, dot_ref[g, h])
                    value_part += mxu(exp_scores.astype(BF16), do_ref[g, h])
                    score_grad = (
                        (SCALE * exp_scores) * (prob_grad - rows_ref[g, 8 + h : 9 + h, :])
                    ).astype(BF16)
                    key_part += mxu(score_grad, q_ref[g, h])
                    dqt_ref[g, h] += mxu(key_t, score_grad)
                acc_ref[:, :HEAD_DIM] += key_part
                acc_ref[:, HEAD_DIM:] += value_part

        dkv_ref[pl.ds(2 * t, 2), slot] = acc_ref[...].astype(BF16).reshape(2, TOKENS, 256)
        return 0

    lax.fori_loop(0, 8, chunk, 0)
    for g in range(2):
        for h in range(MEMBERS):
            columns = slice(h * HEAD_DIM, (h + 1) * HEAD_DIM)
            total = dqt_ref[g, h]
            keep_ref[g, :, columns] = total[:, :TOKENS].T
            send_ref[g, :, columns] = total[:, TOKENS:].T.astype(BF16)


def attention(place, kv, packs, after):
    return pl.pallas_call(
        attention_kernel,
        out_shape=(
            jax.ShapeDtypeStruct((8, 2, TOKENS, 256), BF16),
            jax.ShapeDtypeStruct((2, TOKENS, HALF), F32),
            jax.ShapeDtypeStruct((2, TOKENS, HALF), BF16),
        ),
        in_specs=[pl.BlockSpec(memory_space=pltpu.SMEM)]
        + vmem_specs(5)
        + [pl.BlockSpec(memory_space=pl.ANY)] * len(after),
        out_specs=tuple(vmem_specs(3)),
        scratch_shapes=[
            pltpu.VMEM((2, MEMBERS, 256, HEAD_DIM), BF16),
            pltpu.VMEM((2, MEMBERS, 256, HEAD_DIM), BF16),
            pltpu.VMEM((2, MEMBERS, HEAD_DIM, 256), BF16),
            pltpu.VMEM((2, MEMBERS, HEAD_DIM, 256), BF16),
            pltpu.VMEM((2, MEMBERS, HEAD_DIM, 256), F32),
            pltpu.VMEM((2, 16, 256), F32),
            pltpu.VMEM((256, 256), jnp.int32),
            pltpu.VMEM((256, 256), F32),
        ],
        cost_estimate=pl.CostEstimate(
            flops=16_000_000_000, transcendentals=5_000_000, bytes_accessed=8_000_000
        ),
        compiler_params=pltpu.CompilerParams(vmem_limit_bytes=48 << 20),
        name="attention",
    )(place, kv, *packs, *after)


HALF_COST = 6
KV_COST = 3


def joined_kernel(keep_ref, other_ref, out_ref):
    out_ref[0] = keep_ref[...]
    out_ref[1] = other_ref[...]


def joined(keep, other):
    return pl.pallas_call(
        joined_kernel,
        out_shape=jax.ShapeDtypeStruct((2,) + keep.shape, keep.dtype),
        in_specs=vmem_specs(2),
        out_specs=vmem_specs(1)[0],
        name="joined",
    )(keep, other)


def mark_kernel(_, out_ref):
    out_ref[...] = jnp.zeros_like(out_ref)


def mark(after, cost):
    return pl.pallas_call(
        mark_kernel,
        out_shape=jax.ShapeDtypeStruct((16, HEAD_DIM), BF16),
        in_specs=[ANY],
        out_specs=vmem_specs(1)[0],
        cost_estimate=pl.CostEstimate(
            flops=cost * 1_000_000_000, transcendentals=0, bytes_accessed=1_000_000
        ),
        name="mark",
    )(after)


def half_kernel(first, rows_ref, out_ref):
    out_ref[...] = rows_ref[first : first + 2]


def half(rows, first, cost=HALF_COST):
    shape = (2,) + rows.shape[1:]
    return pl.pallas_call(
        functools.partial(half_kernel, first),
        out_shape=jax.ShapeDtypeStruct(shape, rows.dtype),
        in_specs=vmem_specs(1),
        out_specs=vmem_specs(1)[0],
        cost_estimate=pl.CostEstimate(
            flops=cost * 1_000_000_000, transcendentals=0, bytes_accessed=2_000_000
        ),
        name="half",
    )(rows)


def down_kernel(shards, place_ref, *refs):
    routed, (hidden_ref, out_ref, gathered_ref) = refs[:-3], refs[-3:]
    zl, co = place_ref[0], place_ref[1]

    @pl.when(pl.program_id(0) == 0)
    def _():
        for n, (other_seq, other_z, other_core) in enumerate(shards):
            m = 2 * (1 - zl if other_z else zl) + (1 - co if other_core else co)
            gathered_ref[n] = hidden_ref[:, other_seq, m]

    left_side = gathered_ref[...].reshape(len(shards) * 384, gathered_ref.shape[3])
    right_side = jnp.concatenate([r[...].reshape(-1, out_ref.shape[1]) for r in routed], axis=0)
    out_ref[...] = mxu(left_side, right_side, ((0,), (0,))).astype(BF16)


def down(place, shards, routed, hidden, tile=512):
    width = routed[0].shape[-1]
    rows = hidden.shape[-1]
    whole = lambda i, p: (0, 0, 0, 0, 0)
    return pl.pallas_call(
        functools.partial(down_kernel, shards),
        grid_spec=pltpu.PrefetchScalarGridSpec(
            num_scalar_prefetch=1,
            grid=(width // tile,),
            in_specs=[pl.BlockSpec(r.shape[:2] + (tile,), lambda i, p: (0, 0, i)) for r in routed]
            + [pl.BlockSpec(hidden.shape, whole, pipeline_mode=pl.Buffered(1))],
            out_specs=pl.BlockSpec((rows, tile), lambda i, p: (0, i)),
            scratch_shapes=[pltpu.VMEM((len(shards), 4, 96, rows), BF16)],
        ),
        out_shape=jax.ShapeDtypeStruct((rows, width), BF16),
        cost_estimate=pl.CostEstimate(
            flops=16_000_000_000, transcendentals=0, bytes_accessed=20_000_000
        ),
        compiler_params=pltpu.CompilerParams(vmem_limit_bytes=56 << 20),
        name="down",
    )(place, *routed, hidden)


def finish_kernel(parts_ref, kept_ref, near_ref, mine_ref, send_ref):
    for side, out_ref in ((0, mine_ref), (1, send_ref)):
        out_ref[:, 0:HALF] = (kept_ref[side] + near_ref[side].astype(F32)).astype(BF16)
        total = parts_ref[0, side].astype(F32)
        for part in range(1, 8):
            total = total + parts_ref[part, side].astype(F32)
        out_ref[:, HALF:] = total.astype(BF16)


def finish(parts, kept, near):
    shape = jax.ShapeDtypeStruct((TOKENS, HALF + 256), BF16)
    return pl.pallas_call(
        finish_kernel,
        out_shape=(shape, shape),
        in_specs=vmem_specs(3),
        out_specs=tuple(vmem_specs(2)),
        compiler_params=pltpu.CompilerParams(vmem_limit_bytes=32 << 20),
        name="finish",
    )(parts, kept, near)


def spread_kernel(place_ref, mine_ref, other_ref, _, query_ref, key_ref, value_ref):
    xh = place_ref[0]
    for side, from_ref in ((xh, mine_ref), (1 - xh, other_ref)):
        wide = pl.ds(pl.multiple_of(side * HALF, HEAD_DIM), HALF)
        narrow = pl.ds(pl.multiple_of(side * HEAD_DIM, HEAD_DIM), HEAD_DIM)
        query_ref[:, wide] = from_ref[:, 0:HALF]
        key_ref[:, narrow] = from_ref[:, HALF : HALF + HEAD_DIM]
        value_ref[:, narrow] = from_ref[:, HALF + HEAD_DIM :]


def spread(xh, mine, other, after):
    shape = lambda width: jax.ShapeDtypeStruct((TOKENS, width), BF16)
    return pl.pallas_call(
        spread_kernel,
        out_shape=(shape(2 * HALF), shape(256), shape(256)),
        in_specs=[pl.BlockSpec(memory_space=pltpu.SMEM)] + vmem_specs(2) + [ANY],
        out_specs=tuple(vmem_specs(3)),
        name="spread",
    )(xh[None], mine, other, after)


def local(
    query_rows,
    key_rows,
    value_rows,
    attention_out,
    output_grad,
    log_norms,
    moe_grad,
    expert_ids,
    route_weight,
    hidden_act,
):
    xh, zl, co, dp, tp = (lax.axis_index(name) for name in ("xh", "zl", "co", "dp", "tp"))
    z = lax.axis_index(Z)

    kv_keep, kv_send = pair(xh, key_rows[0], value_rows[0])
    kv = joined(kv_keep, lax.ppermute(kv_send, "xh", SWAP))
    kv_all = lax.all_gather(kv, Z, axis=0)

    corner = lambda arrays: sum(rows[0, :16, :HEAD_DIM] for rows in arrays)

    norms = jnp.pad(log_norms[0].T.reshape(2, MEMBERS, TOKENS), ((0, 0), (0, 2), (0, 0)))
    keep, send, packed = pack(
        xh, query_rows[0], output_grad[0], attention_out[0], norms, kv_keep
    )
    across = lax.ppermute(send, "xh", SWAP)

    outgoing = route(expert_ids[0].T, route_weight[0].T, moe_grad[0], packed)
    routed = lax.all_to_all(outgoing, ("xh", "zq"), 0, 0, tiled=True)
    routed = routed.reshape(4, 2 * CAPACITY, moe_grad.shape[2])
    by_x = lax.ppermute(routed, "dp", SWAP)
    by_z = lax.ppermute(routed, "zl", SWAP)
    diagonal = (lax.ppermute(half(by_z, 0), "dp", SWAP), lax.ppermute(half(by_x, 2), "zl", SWAP))
    shards = (routed, by_x, by_z) + diagonal
    shards += tuple(lax.ppermute(rows, "co", SWAP) for rows in shards)

    hidden = hidden_act[0].reshape(2, 4, CAPACITY, 2048)
    reached = corner([routed, mark(kv_all, KV_COST)[None]])
    keep_half, send_half = halves(dp, hidden, corner([across[None]]) + corner([outgoing]))
    hidden = beside(keep_half, lax.ppermute(send_half, "dp", SWAP), reached)
    hidden = lax.all_gather(hidden, "tp", axis=0)

    packs = (keep, lax.ppermute(keep, "co", SWAP), across, lax.ppermute(across, "co", SWAP))
    dkv, dq_keep, dq_send = attention(
        jnp.stack([xh, z, co]), kv_all, packs, [reached]
    )
    dq_near = lax.ppermute(dq_send, "co", SWAP)
    dkv = lax.all_to_all(dkv, Z, 0, 0, tiled=True)
    mine, send = finish(dkv, dq_keep, dq_near)

    names = tuple((seq, z, core) for core in (0, 1) for seq, z in ((0, 0), (1, 0), (0, 1), (1, 1)))
    down_grad = down(jnp.stack([zl, co]), names, shards, hidden)
    grads = spread(xh, mine, lax.ppermute(send, "xh", SWAP), down_grad)
    return tuple(grad[None] for grad in grads) + (down_grad,)


def solution(mesh):
    fine = Mesh(mesh.devices.reshape(2, 4, 2, 2, 4, 2), ("xh", "zq", "zl", "co", "tp", "dp"))
    cp = ("xh", "zq", "zl", "co")
    return jax.shard_map(
        local,
        mesh=fine,
        in_specs=(
            P("dp", cp, "tp"),
            P("dp", cp, "tp"),
            P("dp", cp, "tp"),
            P("dp", cp, "tp"),
            P("dp", cp, "tp"),
            P("dp", cp, "tp"),
            P("dp", cp, "tp"),
            P("dp", cp, None),
            P("dp", cp, None),
            P("dp", "tp", cp),
        ),
        out_specs=(
            P("dp", cp, "tp"),
            P("dp", cp, "tp"),
            P("dp", cp, "tp"),
            P(cp + ("dp",), "tp"),
        ),
        check_vma=False,
    )
```

```python
import functools

import jax
import jax.numpy as jnp
from jax import lax
from jax.experimental import pallas as pl
from jax.experimental.pallas import tpu as pltpu
from jax.sharding import Mesh, PartitionSpec as P

HEAD_DIM = 128
MEMBERS = 6
EXPERTS = 8
CAPACITY = 48
TOKENS = 128
SCALE = HEAD_DIM ** (-0.5)
LOG2E = 1.4426950408889634
SWAP = [(0, 1), (1, 0)]
Z = ("zq", "zl")
HALF = MEMBERS * HEAD_DIM
F32 = jnp.float32
BF16 = jnp.bfloat16


ANY = pl.BlockSpec(memory_space=pl.ANY)


def vmem_specs(count):
    return [pl.BlockSpec(memory_space=pltpu.VMEM)] * count


def mxu(a, b, contract=((1,), (0,))):
    return lax.dot_general(a, b, (contract, ((), ())), preferred_element_type=F32)


def route_kernel(ids_ref, codes_ref, grad_ref, _, out_ref):
    expert = lax.broadcasted_iota(jnp.int32, (EXPERTS, TOKENS), 0)
    first = expert == ids_ref[0:1, :]
    second = expert == ids_ref[1:2, :]
    real = codes_ref[...].astype(F32) * (1.0 / 32768.0)
    hits = jnp.where(first, 1.0, 0.0) + jnp.where(second, 1.0, 0.0)
    scale = jnp.where(first, real[0:1, :], 0.0) + jnp.where(second, real[1:2, :], 0.0)
    earlier = lax.broadcasted_iota(jnp.int32, (TOKENS, TOKENS), 0)
    later = lax.broadcasted_iota(jnp.int32, (TOKENS, TOKENS), 1)
    before = jnp.where(earlier < later, 1.0, 0.0).astype(BF16)
    rank = mxu(hits.astype(BF16), before)
    rank = jnp.where(hits > 0.0, rank, -1.0)
    slot = lax.broadcasted_iota(jnp.int32, (CAPACITY, TOKENS), 0).astype(F32)
    grads = grad_ref[...]
    for e in range(EXPERTS):
        placed = rank[e : e + 1, :] == slot
        picked = mxu(jnp.where(placed, 1.0, 0.0).astype(BF16), grads)
        weight = jnp.sum(jnp.where(placed, scale[e : e + 1, :], 0.0), axis=1, keepdims=True)
        out_ref[e] = (picked * weight).astype(BF16)


def route(ids, codes, grads, after):
    return pl.pallas_call(
        route_kernel,
        out_shape=jax.ShapeDtypeStruct((EXPERTS, CAPACITY, grads.shape[1]), BF16),
        in_specs=vmem_specs(4),
        out_specs=vmem_specs(1)[0],
        compiler_params=pltpu.CompilerParams(vmem_limit_bytes=32 << 20),
        name="route",
    )(ids, codes, grads, after)


def pair_kernel(place_ref, key_ref, value_ref, keep_ref, send_ref):
    xh = place_ref[0]
    for side, out_ref in ((xh, keep_ref), (1 - xh, send_ref)):
        columns = pl.ds(pl.multiple_of(side * HEAD_DIM, HEAD_DIM), HEAD_DIM)
        out_ref[:, 0:HEAD_DIM] = key_ref[:, columns]
        out_ref[:, HEAD_DIM:] = value_ref[:, columns]


def pair(xh, key, value):
    shape = jax.ShapeDtypeStruct(key.shape, BF16)
    return pl.pallas_call(
        pair_kernel,
        out_shape=(shape, shape),
        in_specs=[pl.BlockSpec(memory_space=pltpu.SMEM)] + vmem_specs(2),
        out_specs=tuple(vmem_specs(2)),
        name="pair",
    )(xh[None], key, value)


def halves_kernel(place_ref, hidden_ref, _, keep_ref, send_ref):
    dp = place_ref[0]
    for side, out_ref in ((dp, keep_ref), (1 - dp, send_ref)):
        columns = pl.ds(pl.multiple_of(side * 1024, 1024), 1024)
        for part in range(2):
            rows = slice(part * CAPACITY, (part + 1) * CAPACITY)
            out_ref[0, rows, :] = hidden_ref[part, 0, :, columns]


def halves(dp, hidden, after):
    shape = jax.ShapeDtypeStruct((4, 2 * CAPACITY, 1024), BF16)
    block = pl.BlockSpec((1, 2 * CAPACITY, 1024), lambda m: (m, 0, 0))
    return pl.pallas_call(
        halves_kernel,
        grid=(4,),
        out_shape=(shape, shape),
        in_specs=[
            pl.BlockSpec(memory_space=pltpu.SMEM),
            pl.BlockSpec((2, 1, CAPACITY, 2048), lambda m: (0, m, 0, 0)),
            pl.BlockSpec(memory_space=pl.ANY),
        ],
        out_specs=(block, block),
        name="halves",
    )(dp[None], hidden, after)


def beside_kernel(keep_ref, other_ref, _, out_ref):
    out_ref[0] = keep_ref[...]
    out_ref[1] = other_ref[...]


def beside(keep, other, after):
    block = pl.BlockSpec((1,) + keep.shape[1:], lambda m: (m, 0, 0))
    return pl.pallas_call(
        beside_kernel,
        grid=keep.shape[:1],
        out_shape=jax.ShapeDtypeStruct((2,) + keep.shape, keep.dtype),
        in_specs=[block, block, ANY],
        out_specs=pl.BlockSpec((2, 1) + keep.shape[1:], lambda m: (0, m, 0, 0)),
        name="beside",
    )(keep, other, after)


def pack_kernel(
    place_ref, query_ref, grad_ref, out_ref, norms_ref, _, keep_ref, send_ref, token_ref, delta_ref
):
    token_ref[...] = jnp.zeros_like(token_ref)
    xh = place_ref[0]
    for head in range(2 * MEMBERS):
        columns = slice(head * HEAD_DIM, (head + 1) * HEAD_DIM)
        product = grad_ref[:, columns].astype(F32) * out_ref[:, columns].astype(F32)
        delta_ref[head // MEMBERS, head % MEMBERS : head % MEMBERS + 1, :] = jnp.sum(
            product.T, axis=0, keepdims=True
        )
    for side, pack_ref in ((xh, keep_ref), (1 - xh, send_ref)):
        columns = pl.ds(pl.multiple_of(side * HALF, HEAD_DIM), HALF)
        pack_ref[0:TOKENS, 0:HALF] = query_ref[:, columns]
        pack_ref[0:TOKENS, HALF : 2 * HALF] = grad_ref[:, columns]
        rest = jnp.concatenate([norms_ref[side] * LOG2E, delta_ref[side]], axis=0)
        pack_ref[TOKENS : TOKENS + 16, :] = jnp.zeros((16, 2 * HALF), BF16)
        for term in range(3):
            part = rest.astype(BF16)
            pack_ref[TOKENS : TOKENS + 16, term * TOKENS : (term + 1) * TOKENS] = part
            rest = rest - part.astype(F32)


def pack(xh, query, grad, out, norms, after):
    shape = jax.ShapeDtypeStruct((TOKENS + 16, query.shape[1]), BF16)
    return pl.pallas_call(
        pack_kernel,
        out_shape=(shape, shape, jax.ShapeDtypeStruct((8, HEAD_DIM), F32)),
        in_specs=[pl.BlockSpec(memory_space=pltpu.SMEM)]
        + vmem_specs(4)
        + [pl.BlockSpec(memory_space=pl.ANY)],
        out_specs=tuple(vmem_specs(3)),
        scratch_shapes=[pltpu.VMEM((2, 8, TOKENS), F32)],
        compiler_params=pltpu.CompilerParams(vmem_limit_bytes=32 << 20),
        name="pack",
    )(xh[None], query, grad, out, norms, after)


def attention_kernel(
    place_ref, kv_ref, p00, p01, p10, p11, *refs
):
    dkv_ref, keep_ref, send_ref = refs[-11:-8]
    q_ref, do_ref, qt_ref, dot_ref, dqt_ref, rows_ref, diff_ref, acc_ref = refs[-8:]
    xh, z, co = place_ref[0], place_ref[1], place_ref[2]
    packs = ((p00, p01), (p10, p11))
    for g in range(2):
        for c in range(2):
            span = slice(c * TOKENS, (c + 1) * TOKENS)
            terms = packs[g][c][TOKENS : TOKENS + 16, 0 : 3 * TOKENS].astype(F32)
            rows_ref[g, :, span] = (
                terms[:, 0:TOKENS] + terms[:, TOKENS : 2 * TOKENS] + terms[:, 2 * TOKENS :]
            )
            for h in range(MEMBERS):
                block = packs[g][c][:TOKENS, h * HEAD_DIM : (h + 1) * HEAD_DIM]
                q_ref[g, h, span, :] = block
                qt_ref[g, h, :, span] = block.T
                block = packs[g][c][:TOKENS, HALF + h * HEAD_DIM : HALF + (h + 1) * HEAD_DIM]
                do_ref[g, h, span, :] = block
                dot_ref[g, h, :, span] = block.T
    dqt_ref[...] = jnp.zeros_like(dqt_ref)
    key_row = lax.broadcasted_iota(jnp.int32, (256, 256), 0)
    query_row = lax.broadcasted_iota(jnp.int32, (256, 256), 1)
    own = query_row < TOKENS
    query_at = jnp.where(own, query_row + co * TOKENS, query_row - TOKENS + (1 - co) * TOKENS)
    diff_ref[...] = query_at - jnp.where(key_row < TOKENS, key_row, key_row + TOKENS)

    def chunk(index, _):
        slot, t = index // 4, index % 4
        xh_key = jnp.where(slot == 0, xh, 1 - xh)
        kv = kv_ref[pl.ds(2 * t, 2), slot].reshape(256, 256)
        key, value = kv[:, :HEAD_DIM], kv[:, HEAD_DIM:]
        key_t = key.T
        acc_ref[...] = jnp.zeros_like(acc_ref)
        for g in range(2):
            xh_query = xh if g == 0 else 1 - xh
            seen = (xh_key < xh_query) | ((xh_key == xh_query) & (t <= z // 2))
            bound = (xh_key - xh_query) * 2048 + t * 512 + co * TOKENS - z * 256

            @pl.when(seen)
            def _():
                key_part = jnp.zeros((256, HEAD_DIM), F32)
                value_part = jnp.zeros((256, HEAD_DIM), F32)
                for h in range(MEMBERS):
                    scores = mxu(key, qt_ref[g, h])
                    exp_scores = jnp.exp2(scores * (SCALE * LOG2E) - rows_ref[g, h : h + 1, :])
                    exp_scores = jnp.where(diff_ref[...] >= bound, exp_scores, 0.0)
                    prob_grad = mxu(value, dot_ref[g, h])
                    value_part += mxu(exp_scores.astype(BF16), do_ref[g, h])
                    score_grad = (
                        (SCALE * exp_scores) * (prob_grad - rows_ref[g, 8 + h : 9 + h, :])
                    ).astype(BF16)
                    key_part += mxu(score_grad, q_ref[g, h])
                    dqt_ref[g, h] += mxu(key_t, score_grad)
                acc_ref[:, :HEAD_DIM] += key_part
                acc_ref[:, HEAD_DIM:] += value_part

        dkv_ref[pl.ds(2 * t, 2), slot] = acc_ref[...].astype(BF16).reshape(2, TOKENS, 256)
        return 0

    lax.fori_loop(0, 8, chunk, 0)
    for g in range(2):
        for h in range(MEMBERS):
            columns = slice(h * HEAD_DIM, (h + 1) * HEAD_DIM)
            total = dqt_ref[g, h]
            keep_ref[g, :, columns] = total[:, :TOKENS].T
            send_ref[g, :, columns] = total[:, TOKENS:].T.astype(BF16)


def attention(place, kv, packs, after):
    return pl.pallas_call(
        attention_kernel,
        out_shape=(
            jax.ShapeDtypeStruct((8, 2, TOKENS, 256), BF16),
            jax.ShapeDtypeStruct((2, TOKENS, HALF), F32),
            jax.ShapeDtypeStruct((2, TOKENS, HALF), BF16),
        ),
        in_specs=[pl.BlockSpec(memory_space=pltpu.SMEM)]
        + vmem_specs(5)
        + [pl.BlockSpec(memory_space=pl.ANY)] * len(after),
        out_specs=tuple(vmem_specs(3)),
        scratch_shapes=[
            pltpu.VMEM((2, MEMBERS, 256, HEAD_DIM), BF16),
            pltpu.VMEM((2, MEMBERS, 256, HEAD_DIM), BF16),
            pltpu.VMEM((2, MEMBERS, HEAD_DIM, 256), BF16),
            pltpu.VMEM((2, MEMBERS, HEAD_DIM, 256), BF16),
            pltpu.VMEM((2, MEMBERS, HEAD_DIM, 256), F32),
            pltpu.VMEM((2, 16, 256), F32),
            pltpu.VMEM((256, 256), jnp.int32),
            pltpu.VMEM((256, 256), F32),
        ],
        cost_estimate=pl.CostEstimate(
            flops=16_000_000_000, transcendentals=5_000_000, bytes_accessed=8_000_000
        ),
        compiler_params=pltpu.CompilerParams(vmem_limit_bytes=48 << 20),
        name="attention",
    )(place, kv, *packs, *after)


PART_COST = 6
KV_COST = 3


def joined_kernel(keep_ref, other_ref, out_ref):
    out_ref[0] = keep_ref[...]
    out_ref[1] = other_ref[...]


def joined(keep, other):
    return pl.pallas_call(
        joined_kernel,
        out_shape=jax.ShapeDtypeStruct((2,) + keep.shape, keep.dtype),
        in_specs=vmem_specs(2),
        out_specs=vmem_specs(1)[0],
        name="joined",
    )(keep, other)


def mark_kernel(_, out_ref):
    out_ref[...] = jnp.zeros_like(out_ref)


def mark(after, cost):
    return pl.pallas_call(
        mark_kernel,
        out_shape=jax.ShapeDtypeStruct((16, HEAD_DIM), BF16),
        in_specs=[ANY],
        out_specs=vmem_specs(1)[0],
        cost_estimate=pl.CostEstimate(
            flops=cost * 1_000_000_000, transcendentals=0, bytes_accessed=1_000_000
        ),
        name="mark",
    )(after)


def part_kernel(rows, rows_ref, out_ref):
    out_ref[...] = rows_ref[rows]


def part(array, rows):
    shape = (rows.stop - rows.start,) + array.shape[1:]
    return pl.pallas_call(
        functools.partial(part_kernel, rows),
        out_shape=jax.ShapeDtypeStruct(shape, array.dtype),
        in_specs=vmem_specs(1),
        out_specs=vmem_specs(1)[0],
        cost_estimate=pl.CostEstimate(
            flops=PART_COST * 1_000_000_000, transcendentals=0, bytes_accessed=2_000_000
        ),
        name="part",
    )(array)


def down_kernel(shards, place_ref, *refs):
    routed, (hidden_ref, out_ref, gathered_ref) = refs[:-3], refs[-3:]
    zl, co = place_ref[0], place_ref[1]

    @pl.when(pl.program_id(0) == 0)
    def _():
        for n, (other_seq, other_z, other_core) in enumerate(shards):
            m = 2 * (1 - zl if other_z else zl) + (1 - co if other_core else co)
            gathered_ref[n] = hidden_ref[:, other_seq, m]

    left_side = gathered_ref[...].reshape(len(shards) * 384, gathered_ref.shape[3])
    right_side = jnp.concatenate([r[...].reshape(-1, out_ref.shape[1]) for r in routed], axis=0)
    out_ref[...] = mxu(left_side, right_side, ((0,), (0,))).astype(BF16)


def down(place, shards, routed, hidden, tile=512):
    width = routed[0].shape[-1]
    rows = hidden.shape[-1]
    whole = lambda i, p: (0, 0, 0, 0, 0)
    return pl.pallas_call(
        functools.partial(down_kernel, shards),
        grid_spec=pltpu.PrefetchScalarGridSpec(
            num_scalar_prefetch=1,
            grid=(width // tile,),
            in_specs=[pl.BlockSpec(r.shape[:2] + (tile,), lambda i, p: (0, 0, i)) for r in routed]
            + [pl.BlockSpec(hidden.shape, whole, pipeline_mode=pl.Buffered(1))],
            out_specs=pl.BlockSpec((rows, tile), lambda i, p: (0, i)),
            scratch_shapes=[pltpu.VMEM((len(shards), 4, 96, rows), BF16)],
        ),
        out_shape=jax.ShapeDtypeStruct((rows, width), BF16),
        cost_estimate=pl.CostEstimate(
            flops=16_000_000_000, transcendentals=0, bytes_accessed=20_000_000
        ),
        compiler_params=pltpu.CompilerParams(vmem_limit_bytes=56 << 20),
        name="down",
    )(place, *routed, hidden)


def finish_kernel(parts_ref, kept_ref, near_ref, mine_ref, send_ref):
    for side, out_ref in ((0, mine_ref), (1, send_ref)):
        out_ref[:, 0:HALF] = (kept_ref[side] + near_ref[side].astype(F32)).astype(BF16)
        total = parts_ref[0, side].astype(F32)
        for part in range(1, 8):
            total = total + parts_ref[part, side].astype(F32)
        out_ref[:, HALF:] = total.astype(BF16)


def finish(parts, kept, near):
    shape = jax.ShapeDtypeStruct((TOKENS, HALF + 256), BF16)
    return pl.pallas_call(
        finish_kernel,
        out_shape=(shape, shape),
        in_specs=vmem_specs(3),
        out_specs=tuple(vmem_specs(2)),
        compiler_params=pltpu.CompilerParams(vmem_limit_bytes=32 << 20),
        name="finish",
    )(parts, kept, near)


def spread_kernel(place_ref, mine_ref, other_ref, _, query_ref, key_ref, value_ref):
    xh = place_ref[0]
    for side, from_ref in ((xh, mine_ref), (1 - xh, other_ref)):
        wide = pl.ds(pl.multiple_of(side * HALF, HEAD_DIM), HALF)
        narrow = pl.ds(pl.multiple_of(side * HEAD_DIM, HEAD_DIM), HEAD_DIM)
        query_ref[:, wide] = from_ref[:, 0:HALF]
        key_ref[:, narrow] = from_ref[:, HALF : HALF + HEAD_DIM]
        value_ref[:, narrow] = from_ref[:, HALF + HEAD_DIM :]


def spread(xh, mine, other, after):
    shape = lambda width: jax.ShapeDtypeStruct((TOKENS, width), BF16)
    return pl.pallas_call(
        spread_kernel,
        out_shape=(shape(2 * HALF), shape(256), shape(256)),
        in_specs=[pl.BlockSpec(memory_space=pltpu.SMEM)] + vmem_specs(2) + [ANY],
        out_specs=tuple(vmem_specs(3)),
        name="spread",
    )(xh[None], mine, other, after)


def local(
    query_rows,
    key_rows,
    value_rows,
    attention_out,
    output_grad,
    log_norms,
    moe_grad,
    expert_ids,
    route_weight,
    hidden_act,
):
    xh, zl, co, dp, tp = (lax.axis_index(name) for name in ("xh", "zl", "co", "dp", "tp"))
    z = lax.axis_index(Z)

    kv_keep, kv_send = pair(xh, key_rows[0], value_rows[0])
    kv = joined(kv_keep, lax.ppermute(kv_send, "xh", SWAP))
    kv_all = lax.all_gather(kv, Z, axis=0)

    corner = lambda arrays: sum(rows[0, :16, :HEAD_DIM] for rows in arrays)

    norms = jnp.pad(log_norms[0].T.reshape(2, MEMBERS, TOKENS), ((0, 0), (0, 2), (0, 0)))
    keep, send, packed = pack(
        xh, query_rows[0], output_grad[0], attention_out[0], norms, kv_keep
    )
    across = lax.ppermute(send, "xh", SWAP)

    outgoing = route(expert_ids[0].T, route_weight[0].T, moe_grad[0], packed)
    routed = lax.all_to_all(outgoing, ("xh", "zq"), 0, 0, tiled=True)
    routed = routed.reshape(4, 2 * CAPACITY, moe_grad.shape[2])
    by_x = lax.ppermute(routed, "dp", SWAP)
    by_z = lax.ppermute(routed, "zl", SWAP)
    diagonal = (
        lax.ppermute(part(by_z, slice(0, 2)), "dp", SWAP),
        lax.ppermute(part(by_x, slice(2, 4)), "zl", SWAP),
    )
    shards = (routed, by_x, by_z) + diagonal
    shards += tuple(lax.ppermute(rows, "co", SWAP) for rows in shards)

    hidden = hidden_act[0].reshape(2, 4, CAPACITY, 2048)
    reached = corner([routed, mark(kv_all, KV_COST)[None], across[None]])
    keep_half, send_half = halves(dp, hidden, corner([outgoing]))
    hidden = beside(keep_half, lax.ppermute(send_half, "dp", SWAP), reached)
    hidden = lax.all_gather(hidden, "tp", axis=0)

    packs = (keep, lax.ppermute(keep, "co", SWAP), across, lax.ppermute(across, "co", SWAP))
    dkv, dq_keep, dq_send = attention(
        jnp.stack([xh, z, co]), kv_all, packs, [reached]
    )
    dq_near = lax.ppermute(dq_send, "co", SWAP)
    dkv = lax.all_to_all(dkv, Z, 0, 0, tiled=True)
    mine, send = finish(dkv, dq_keep, dq_near)

    names = tuple((seq, z, core) for core in (0, 1) for seq, z in ((0, 0), (1, 0), (0, 1), (1, 1)))
    down_grad = down(jnp.stack([zl, co]), names, shards, hidden)
    grads = spread(xh, mine, lax.ppermute(send, "xh", SWAP), down_grad)
    return tuple(grad[None] for grad in grads) + (down_grad,)


def solution(mesh):
    fine = Mesh(mesh.devices.reshape(2, 4, 2, 2, 4, 2), ("xh", "zq", "zl", "co", "tp", "dp"))
    cp = ("xh", "zq", "zl", "co")
    return jax.shard_map(
        local,
        mesh=fine,
        in_specs=(
            P("dp", cp, "tp"),
            P("dp", cp, "tp"),
            P("dp", cp, "tp"),
            P("dp", cp, "tp"),
            P("dp", cp, "tp"),
            P("dp", cp, "tp"),
            P("dp", cp, "tp"),
            P("dp", cp, None),
            P("dp", cp, None),
            P("dp", "tp", cp),
        ),
        out_specs=(
            P("dp", cp, "tp"),
            P("dp", cp, "tp"),
            P("dp", cp, "tp"),
            P(cp + ("dp",), "tp"),
        ),
        check_vma=False,
    )
```
